512 devices in a mesh: group: 8 (over x, core), ctx: 64 (over y, z).
Axes of the slice: x: 4, y: 4, z: 16, core: 2. Of those that a mesh axis runs over, the one named last changes fastest.
Arguments:
- projected_queries: bfloat16 [65536, 4096], P(('group', 'ctx')), may hold values from -6 to 6
- projected_keys: bfloat16 [65536, 4096], P(('group', 'ctx')), may hold values from -6 to 6
- projected_values: bfloat16 [65536, 4096], P(('group', 'ctx')), may hold values from -6 to 6
- short_filter_taps: float32 [3, 3, 4096], P(None, None, 'ctx'), may hold values from -3.5 to 3.5
- long_filter_taps: bfloat16 [128, 4096], P(None, 'ctx'), may hold values from -0.5 to 0.5
- adapter_down_weight: bfloat16 [256, 16, 4096], P('ctx', None, 'group'), may hold values from -0.09375 to 0.09375
- adapter_up_weight: bfloat16 [256, 16, 4096], P('ctx', None, 'group'), may hold values from -0.5 to 0.5
- slab_adapter_index: int32 [8, 8], P('group'), may hold values from 0 to 255
- adapter_owner_slot: int32 [256], replicated, may hold values from 0 to 255, each once
Outputs:
- adapted: bfloat16 [65536, 4096], P(('group', 'ctx'))
The draws below stay inside these ranges and needn't reach their ends.
Inputs may be any that keep to these rules, and one draw needn't show every extreme that they name: `slab_adapter_index`: a slab's list may name an adapter more than once. `adapter_owner_slot`: each slot once.
All inputs are finite; a program needn't handle non-finite values.
Results may differ from the reference program's by a relative error of at most 0.0054.
Values may be sent and summed in bfloat16 or wider, within the bound.
A program may use at most 64 MiB of HBM per device.

```python
import math
import jax
import jax.numpy as jnp
import numpy as np
from jax import lax

STREAM_WIDTH = 4096
ADAPTER_RANK = 16
FIR = 3
FLEN = 128
LIST_LENGTH = 8
ADAPTER_TOTAL = 256
SLAB = 8192
GROUPS = 8
TOKENS = 65536


def touch_ends(drawn, key, low, high):
    dims = drawn.shape
    place = [jax.random.randint(jax.random.fold_in(key, axis), (), 0, dims[axis]) for axis in range(len(dims))]
    drawn = drawn.at[tuple(place)].set(low)
    longest = dims.index(max(dims))
    place[longest] = (place[longest] + 1) % dims[longest]
    return drawn.at[tuple(place)].set(high)


def block_scale(rng, shape, cuts, smallest, top_value):
    gain = 1.0
    for axis_at, blocks in cuts:
        draws = jax.random.uniform(jax.random.fold_in(jax.random.fold_in(rng, 6), axis_at), (blocks,), jnp.float32, smallest / len(cuts), top_value / len(cuts))
        gain = gain * jnp.repeat(jnp.exp(draws), shape[axis_at] // blocks).reshape((-1,) + (1,) * (len(shape) - 1 - axis_at))
    return gain


def rank_bounds(number_of, lean):
    portions = [(1 << 20) // math.isqrt(grade ** lean) + 1 for grade in range(1, number_of + 1)]
    deviation = 1 + sum(portions) // (1 << 30)
    return np.cumsum(np.array([max(1, weight // deviation) for weight in portions]))


def ranked(key, extent, amount, skew):
    listing = rank_bounds(amount, skew)
    pick = jax.random.randint(jax.random.fold_in(key, 1), extent, 0, int(listing[amount - 1]))
    rank = jnp.searchsorted(jnp.asarray(listing, jnp.int32), pick, side="right")
    return jax.random.permutation(jax.random.fold_in(key, 2), amount)[rank].astype(jnp.int32)


def bell_draw(key, extent, spread, limit, pieces=(), held_as=jnp.bfloat16):
    values = spread * jax.random.normal(key, extent, jnp.float32)
    if pieces:
        values = values * block_scale(key, extent, pieces, -0.22, 0.18)
    return jnp.clip(values, -limit, limit).astype(held_as)


def setup_inputs(seed: int = 0) -> dict:
    key_of = jax.random.split(jax.random.key(seed), 10)
    return {
        "projected_queries": bell_draw(key_of[0], (TOKENS, STREAM_WIDTH), 1.0, 6.0, ((0, 512),)),
        "projected_keys": bell_draw(key_of[1], (TOKENS, STREAM_WIDTH), 1.0, 6.0, ((0, 512),)),
        "projected_values": bell_draw(key_of[2], (TOKENS, STREAM_WIDTH), 1.0, 6.0, ((0, 512),)),
        "short_filter_taps": bell_draw(key_of[3], (3, FIR, STREAM_WIDTH), FIR ** -0.5, 3.5, ((2, 64),), jnp.float32),
        "long_filter_taps": bell_draw(key_of[4], (FLEN, STREAM_WIDTH), FLEN ** -0.5, 0.5, ((1, 64),)),
        "adapter_down_weight": bell_draw(key_of[5], (ADAPTER_TOTAL, ADAPTER_RANK, STREAM_WIDTH), STREAM_WIDTH ** -0.5, 0.09375, ((0, 64), (2, 8))),
        "adapter_up_weight": bell_draw(key_of[6], (ADAPTER_TOTAL, ADAPTER_RANK, STREAM_WIDTH), (LIST_LENGTH * ADAPTER_RANK) ** -0.5, 0.5, ((0, 64), (2, 8))),
        "slab_adapter_index": touch_ends(ranked(key_of[7], (GROUPS, LIST_LENGTH), ADAPTER_TOTAL, 2), jax.random.fold_in(key_of[7], 3), 0, ADAPTER_TOTAL - 1).astype(jnp.int32),
        "adapter_owner_slot": jax.random.permutation(key_of[8], ADAPTER_TOTAL).astype(jnp.int32),
    }


def taps_apply(signal, taps):
    count = signal.shape[0]
    width = taps.shape[0]
    padded = jnp.pad(signal, ((width - 1, 0), (0, 0)))
    total = jnp.zeros_like(signal)
    for offset in range(width):
        total = total + taps[offset] * padded[width - 1 - offset: width - 1 - offset + count]
    return total


def reference(projected_queries, projected_keys, projected_values, short_filter_taps, long_filter_taps, adapter_down_weight, adapter_up_weight, slab_adapter_index, adapter_owner_slot):
    length = 2 * SLAB
    filter_freq = jnp.fft.rfft(long_filter_taps.astype(jnp.float32), n=length, axis=0)

    def one_slab(items):
        query, keys, values, listed = items
        q_short = taps_apply(query.astype(jnp.float32), short_filter_taps[0])
        k_short = taps_apply(keys.astype(jnp.float32), short_filter_taps[1])
        v_short = taps_apply(values.astype(jnp.float32), short_filter_taps[2])
        gated = k_short * v_short
        spectrum = jnp.fft.rfft(gated, n=length, axis=0) * filter_freq
        long_conv = jnp.fft.irfft(spectrum, n=length, axis=0)[:SLAB].astype(jnp.float32)
        mixed = (q_short * long_conv).astype(jnp.bfloat16)
        holder_slots = adapter_owner_slot[listed]
        joined_down_maps = adapter_down_weight[holder_slots].reshape(LIST_LENGTH * ADAPTER_RANK, STREAM_WIDTH)
        joined_up_maps = adapter_up_weight[holder_slots].reshape(LIST_LENGTH * ADAPTER_RANK, STREAM_WIDTH)
        low = jnp.dot(mixed, joined_down_maps.T, preferred_element_type=jnp.float32).astype(jnp.bfloat16)
        total = mixed.astype(jnp.float32) + jnp.dot(low, joined_up_maps, preferred_element_type=jnp.float32)
        return total.astype(jnp.bfloat16)

    slabs = (projected_queries.reshape(GROUPS, SLAB, STREAM_WIDTH), projected_keys.reshape(GROUPS, SLAB, STREAM_WIDTH),
             projected_values.reshape(GROUPS, SLAB, STREAM_WIDTH), slab_adapter_index)
    adapted = lax.map(one_slab, slabs)
    return adapted.reshape(TOKENS, STREAM_WIDTH)
```

```python
import jax
import jax.numpy as jnp
import numpy as np
from jax import lax
from jax.experimental import pallas as pl
from jax.experimental.pallas import tpu as pltpu
from jax.sharding import PartitionSpec as P

MESH = pl.DeviceIdType.MESH
BF = jnp.bfloat16
F32 = jnp.float32
ROWS = 128
WIDTH = 4096
CHUNK = 512
CHUNKS = WIDTH // CHUNK
POINTS = 256
HALF = POINTS // 2


def split_high_low(matrix):
    high = matrix.astype(jnp.bfloat16)
    low = (matrix - high.astype(np.float64)).astype(jnp.bfloat16)
    return high, low


def transforms():
    row = np.arange(POINTS)
    angle = 2 * np.pi * np.outer(np.arange(HALF), row) / POINTS
    sine = -np.sin(angle)
    sine[0] = (-1.0) ** row
    forward = np.concatenate([np.cos(angle), sine], axis=0)
    back_cos = np.cos(angle[:, HALF:]).T * (2 / POINTS)
    back_cos[:, 0] = 1 / POINTS
    back_sine = -np.sin(angle[:, HALF:]).T * (2 / POINTS)
    back_sine[:, 0] = (-1.0) ** row[HALF:] / POINTS
    back = np.concatenate([back_cos, back_sine], axis=1)
    return split_high_low(forward) + split_high_low(back)


def place(y, z):
    return y * 16 + (z % 4) * 4 + z // 4


def dot(a, b):
    return lax.dot_general(a, b, (((1,), (0,)), ((), ())), preferred_element_type=F32)


def dot_nt(a, b):
    return lax.dot_general(a, b, (((1,), (1,)), ((), ())), preferred_element_type=F32)


def mixer_kernel(
    slots_ref, q_ref, k_ref, v_ref, tail_ref, short_ref, long_ref, down_ref, up_ref,
    fwd_hi, fwd_lo, back_hi, back_lo,
    out_ref,
    bank_d, bank_u, send_x, recv_x, part_b, sum_b, part_a, sum_a, fin,
    first_s, first_l, short_all, long_all, even_taps, odd_taps, tails, halo,
    gate_hi, gate_lo, spectrum, filt_re, filt_im, filt_re2, q_short, mixed,
    local_sem, tail_sem, halo_send, halo_recv, f_send, f_recv, a_send, a_recv,
):
    group = lax.axis_index("group")
    ctx = lax.axis_index("ctx")
    x, core = group // 2, group % 2
    y, z = ctx // 16, ctx % 16
    z_low, z_high = z % 4, z // 4
    has_before = ctx > 0

    def at_y(d):
        return (group, ((y + d) % 4) * 16 + z)

    def at_z(d):
        return (group, y * 16 + (z + d + 16) % 16)

    def at_x(d):
        return (((x + d) % 4) * 2 + core, ctx)

    def at_group(d):
        return ((group + d) % 8, ctx)

    after = (group, (ctx + 1) % 64)
    before = (group, (ctx + 63) % 64)

    barrier = pltpu.get_barrier_semaphore()
    peers = [at_y(d) for d in (1, 2, 3)] + [at_group(d) for d in range(1, 8)]
    peers += [at_z(d) for d in (1, -1, 2, -2, 4, -4, 8)] + [after, before]
    for peer in peers:
        pl.semaphore_signal(barrier, inc=1, device_id=peer, device_id_type=MESH)
    pl.semaphore_wait(barrier, len(peers))

    pending = []
    used = {"f": 0, "a": 0}

    def send(kind, src, dst, peer):
        at = used[kind]
        used[kind] += 1
        sems = (f_send, f_recv) if kind == "f" else (a_send, a_recv)
        copy = pltpu.make_async_remote_copy(
            src, dst, sems[0].at[at], sems[1].at[at], device_id=peer, device_id_type=MESH
        )
        copy.start()
        pending.append(copy)
        return copy

    def arrived(copies):
        for copy in copies:
            copy.wait_recv()

    tail_copy = pltpu.make_async_remote_copy(
        tail_ref, tails, tail_sem.at[0], tail_sem.at[1], device_id=after, device_id_type=MESH
    )
    tail_copy.start()
    round_f1 = []
    for d in (1, 2, 3):
        round_f1.append(send("f", short_ref, first_s.at[y], at_y(d)))
        round_f1.append(send("f", long_ref, first_l.at[y], at_y(d)))
    round_a1 = []
    for d in (1, 2, 3):
        round_a1.append(send("a", down_ref, bank_d.at[y], at_y(d)))
        round_a1.append(send("a", up_ref, bank_u.at[y], at_y(d)))
    first_s[y] = short_ref[...]
    first_l[y] = long_ref[...]
    bank_d[y] = down_ref[...]
    bank_u[y] = up_ref[...]

    arrived(round_f1)
    mine = place(x, z)
    round_f2 = []
    for d in (4, 8, -4):
        round_f2.append(send("f", first_s.at[x], short_all.at[mine], at_z(d)))
    for d in (4, 8, -4):
        round_f2.append(send("f", first_l.at[x], long_all.at[mine], at_z(d)))
    short_all[mine] = first_s[x]
    long_all[mine] = first_l[x]

    arrived(round_a1)
    round_a2 = []
    for d in range(8):
        slab = (group + d) % 8
        for e in range(2):
            slot = slots_ref[slab, y + 4 * e]
            keep = ((slot // 4) % 16 == z).astype(F32)
            down_one = (bank_d[slot // 64, slot % 4].astype(F32) * keep).astype(BF)
            up_one = (bank_u[slot // 64, slot % 4].astype(F32) * keep).astype(BF)
            if d == 0:
                recv_x[e, group] = down_one
                recv_x[2 + e, group] = up_one
            else:
                send_x[d - 1, e] = down_one
                send_x[d - 1, 2 + e] = up_one
        if d:
            round_a2.append(send("a", send_x.at[d - 1], recv_x.at[:, group], at_group(d)))

    arrived(round_f2)
    quad = pl.ds(x * 16 + z_low * 4, 4)
    round_f3 = []
    for d in (1, -1, -2):
        round_f3.append(send("f", short_all.at[quad], short_all.at[quad], at_z(d)))
    for d in (1, -1, -2):
        round_f3.append(send("f", long_all.at[quad], long_all.at[quad], at_z(d)))

    arrived(round_a2)
    round_a3 = []
    for j, d in enumerate((1, -1, -2)):
        round_a3.append(send("a", recv_x.at[(z + d + 16) % 4], part_b.at[j], at_z(d)))

    arrived(round_f3)
    row16 = pl.ds(x * 16, 16)
    round_f4s = []
    for d in (1, 2, 3):
        round_f4s.append(send("f", short_all.at[row16], short_all.at[row16], at_x(d)))
    round_f4l = []
    for d in (1, 2, 3):
        round_f4l.append(send("f", long_all.at[row16], long_all.at[row16], at_x(d)))

    arrived(round_a3)
    for c in range(8):
        sum_b[c] = (
            recv_x[z_low, c].astype(F32) + part_b[0, c].astype(F32)
            + part_b[1, c].astype(F32) + part_b[2, c].astype(F32)
        ).astype(BF)
    round_a4 = []
    for j in (1, 2, 3):
        cols = pl.ds(pl.multiple_of(((z_high + j) % 4) * 128, 128), 128)
        round_a4.append(send("a", sum_b.at[:, :, cols], part_a.at[j - 1], at_z(4 * j)))

    tail_copy.wait_recv()
    arrived(round_f4s)
    lane = lax.broadcasted_iota(jnp.int32, (8, 128), 1)

    def unpack(m, carry):
        h = 2 * m
        one = short_all[place(h // 16, h % 16)]
        two = short_all[place((h + 1) // 16, (h + 1) % 16)]
        at = pl.ds(pl.multiple_of(m * 128, 128), 128)
        even_taps[:, at] = jnp.where(lane < 64, one, pltpu.roll(two, 64, 1))
        odd_taps[:, at] = jnp.where(lane < 64, pltpu.roll(one, 64, 1), two)
        return carry

    lax.fori_loop(0, WIDTH // 128, unpack, 0)
    row = lax.broadcasted_iota(jnp.int32, (ROWS, CHUNK), 0)

    def short_filter(ref, stream, at):
        signal = ref[:, at].astype(F32)
        edge = jnp.where(has_before, tails[:, at].astype(F32), 0.0)
        older, newer = edge[2 * stream:2 * stream + 1], edge[2 * stream + 1:2 * stream + 2]
        back1 = jnp.where(row == 0, newer, pltpu.roll(signal, 1, 0))
        back2 = jnp.where(row == 0, older, jnp.where(row == 1, newer, pltpu.roll(signal, 2, 0)))
        total = None
        for j, shifted in enumerate((signal, back1, back2)):
            n = 3 * stream + j
            taps = (even_taps if n % 2 == 0 else odd_taps)[n // 2:n // 2 + 1, at]
            total = taps * shifted if total is None else total + taps * shifted
        return total

    def columns(c):
        return pl.ds(pl.multiple_of(c * CHUNK, CHUNK), CHUNK)

    def halo_copy(c):
        at = columns(c)
        return pltpu.make_async_remote_copy(
            gate_hi.at[:, at], halo.at[:, at], halo_send.at[c], halo_recv.at[c],
            device_id=after, device_id_type=MESH,
        )

    def gate(c, carry):
        at = columns(c)
        gated = short_filter(k_ref, 1, at) * short_filter(v_ref, 2, at)
        high = gated.astype(BF)
        gate_hi[:, at] = high
        gate_lo[:, at] = (gated - high.astype(F32)).astype(BF)
        halo_copy(c).start()
        return carry

    lax.fori_loop(0, CHUNKS, gate, 0)

    arrived(round_a4)
    own = pl.ds(pl.multiple_of(z_high * 128, 128), 128)
    for c in range(8):
        total = (
            sum_b[c, :, own].astype(F32) + part_a[0, c].astype(F32)
            + part_a[1, c].astype(F32) + part_a[2, c].astype(F32)
        ).astype(BF)
        sum_a[c] = total
        fin[z_low, y, c, :, own] = total
    round_a5 = []
    for j in (1, 2, 3):
        round_a5.append(send("a", sum_a, fin.at[z_low, y, :, :, own], at_z(4 * j)))

    arrived(round_f4l)

    def own_rows(c, carry):
        at = columns(c)
        q_short[:, at] = short_filter(q_ref, 0, at)
        high, low = gate_hi[:, at], gate_lo[:, at]
        spectrum[:, at] = (
            dot(fwd_hi[:, HALF:], high) + dot(fwd_lo[:, HALF:], high) + dot(fwd_hi[:, HALF:], low)
        )
        blocks = []
        for i in range(8):
            blocks.append(long_all[place(c // 2, 8 * (c % 2) + i)])
        taps = jnp.concatenate(blocks, axis=0)
        filt = dot_nt(fwd_hi[:, :HALF], taps) + dot_nt(fwd_lo[:, :HALF], taps)
        re, im = filt[:HALF], filt[HALF:]
        filt_re[:, at] = re
        filt_im[:, at] = jnp.where(row == 0, 0.0, im)
        filt_re2[:, at] = jnp.where(row == 0, im, re)
        return carry

    lax.fori_loop(0, 4, own_rows, 0)
    arrived(round_a5)
    round_a6 = []
    for d in (1, -1, -2):
        round_a6.append(send("a", fin.at[z_low, y], fin.at[z_low, y], at_z(d)))
    round_a7 = []
    for d in (1, 2, 3):
        round_a7.append(send("a", fin.at[z_low, y], fin.at[z_low, y], at_y(d)))
    lax.fori_loop(4, CHUNKS, own_rows, 0)
    for copy, d in zip(round_a6, (-1, 1, 2)):
        copy.wait_recv()
        k = (z + d + 16) % 4
        for e in (1, 2, 3):
            round_a7.append(send("a", fin.at[k, y], fin.at[k, y], at_y(e)))

    def mix(c, carry):
        at = columns(c)
        halo_copy(c).wait_recv()
        old = jnp.where(has_before, halo[:, at].astype(F32), 0.0).astype(BF)
        total = spectrum[:, at] + dot(fwd_hi[:, :HALF], old) + dot(fwd_lo[:, :HALF], old)
        re, im = total[:HALF], total[HALF:]
        f_im = filt_im[:, at]
        prod_re = re * filt_re[:, at] - im * f_im
        prod_im = re * f_im + im * filt_re2[:, at]
        re_hi, im_hi = prod_re.astype(BF), prod_im.astype(BF)
        re_lo = (prod_re - re_hi.astype(F32)).astype(BF)
        im_lo = (prod_im - im_hi.astype(F32)).astype(BF)
        high = jnp.concatenate([re_hi, im_hi], axis=0)
        low = jnp.concatenate([re_lo, im_lo], axis=0)
        long_conv = dot(back_hi[...], high) + dot(back_lo[...], high) + dot(back_hi[...], low)
        mixed[:, at] = (q_short[:, at] * long_conv).astype(BF)
        return carry

    lax.fori_loop(0, CHUNKS, mix, 0)

    arrived(round_a7)

    def down(c, total):
        maps = fin[pl.ds(0, 2), :, c].reshape(ROWS, CHUNK)
        return total + dot_nt(mixed[:, columns(c)], maps)

    low_rank = lax.fori_loop(0, CHUNKS, down, jnp.zeros((ROWS, ROWS), F32)).astype(BF)

    def up(c, carry):
        maps = fin[pl.ds(2, 2), :, c].reshape(ROWS, CHUNK)
        at = columns(c)
        out_ref[:, at] = (mixed[:, at].astype(F32) + dot(low_rank, maps)).astype(BF)
        return carry

    lax.fori_loop(0, CHUNKS, up, 0)

    tail_copy.wait_send()
    for copy in pending:
        copy.wait_send()

    def drain(c, carry):
        halo_copy(c).wait_send()
        return carry

    lax.fori_loop(0, CHUNKS, drain, 0)


def on_device(
    projected_queries,
    projected_keys,
    projected_values,
    short_filter_taps,
    long_filter_taps,
    adapter_down_weight,
    adapter_up_weight,
    slab_adapter_index,
    adapter_owner_slot,
):
    listed = lax.all_gather(slab_adapter_index, "group", axis=0, tiled=True)
    bank = jnp.arange(adapter_owner_slot.shape[0], dtype=jnp.int32)
    slots = jnp.sum(
        jnp.where(listed[:, :, None] == bank, adapter_owner_slot[None, None, :], 0), axis=2
    )
    tail = jnp.concatenate(
        [projected_queries[ROWS - 2:], projected_keys[ROWS - 2:], projected_values[ROWS - 2:]]
        + [jnp.zeros((10, WIDTH), BF)],
        axis=0,
    )
    short = jnp.pad(short_filter_taps.reshape(9, 64), ((0, 7), (0, 0))).reshape(8, 128)
    constants = [jnp.asarray(part) for part in transforms()]
    vmem = pl.BlockSpec(memory_space=pltpu.VMEM)
    return pl.pallas_call(
        mixer_kernel,
        out_shape=jax.ShapeDtypeStruct((ROWS, WIDTH), BF),
        in_specs=[pl.BlockSpec(memory_space=pltpu.SMEM)] + [vmem] * 12,
        out_specs=vmem,
        scratch_shapes=[
            pltpu.VMEM((4, 4, 16, CHUNK), BF),
            pltpu.VMEM((4, 4, 16, CHUNK), BF),
            pltpu.VMEM((7, 4, 16, CHUNK), BF),
            pltpu.VMEM((4, 8, 16, CHUNK), BF),
            pltpu.VMEM((3, 8, 16, CHUNK), BF),
            pltpu.VMEM((8, 16, CHUNK), BF),
            pltpu.VMEM((3, 8, 16, 128), BF),
            pltpu.VMEM((8, 16, 128), BF),
            pltpu.VMEM((4, 4, 8, 16, CHUNK), BF),
            pltpu.VMEM((4, 8, 128), F32),
            pltpu.VMEM((4, 64, 128), BF),
            pltpu.VMEM((64, 8, 128), F32),
            pltpu.VMEM((64, 64, 128), BF),
            pltpu.VMEM((8, WIDTH), F32),
            pltpu.VMEM((8, WIDTH), F32),
            pltpu.VMEM((16, WIDTH), BF),
            pltpu.VMEM((ROWS, WIDTH), BF),
            pltpu.VMEM((ROWS, WIDTH), BF),
            pltpu.VMEM((ROWS, WIDTH), BF),
            pltpu.VMEM((POINTS, WIDTH), F32),
            pltpu.VMEM((HALF, WIDTH), F32),
            pltpu.VMEM((HALF, WIDTH), F32),
            pltpu.VMEM((HALF, WIDTH), F32),
            pltpu.VMEM((ROWS, WIDTH), F32),
            pltpu.VMEM((ROWS, WIDTH), BF),
            pltpu.SemaphoreType.DMA((2,)),
            pltpu.SemaphoreType.DMA((2,)),
            pltpu.SemaphoreType.DMA((CHUNKS,)),
            pltpu.SemaphoreType.DMA((CHUNKS,)),
            pltpu.SemaphoreType.DMA((24,)),
            pltpu.SemaphoreType.DMA((24,)),
            pltpu.SemaphoreType.DMA((37,)),
            pltpu.SemaphoreType.DMA((37,)),
        ],
        compiler_params=pltpu.CompilerParams(
            collective_id=0, has_side_effects=True, vmem_limit_bytes=56 * 1024 * 1024
        ),
        cost_estimate=pl.CostEstimate(
            flops=3_000_000_000, bytes_accessed=8_000_000, transcendentals=0
        ),
    )(
        slots, projected_queries, projected_keys, projected_values, tail, short,
        long_filter_taps.T, adapter_down_weight, adapter_up_weight, *constants,
    )


def solution(mesh):
    in_specs = (
        P(("group", "ctx"), None),
        P(("group", "ctx"), None),
        P(("group", "ctx"), None),
        P(None, None, "ctx"),
        P(None, "ctx"),
        P("ctx", None, "group"),
        P("ctx", None, "group"),
        P("group", None),
        P(),
    )
    out_specs = P(("group", "ctx"), None)
    return jax.shard_map(
        on_device, mesh=mesh, in_specs=in_specs, out_specs=out_specs, check_vma=False
    )
```

```python
import jax
import jax.numpy as jnp
import numpy as np
from jax import lax
from jax.experimental import pallas as pl
from jax.experimental.pallas import tpu as pltpu
from jax.sharding import PartitionSpec as P

MESH = pl.DeviceIdType.MESH
BF = jnp.bfloat16
F32 = jnp.float32
ROWS = 128
WIDTH = 4096
CHUNK = 512
CHUNKS = WIDTH // CHUNK
POINTS = 256
HALF = POINTS // 2


def split_high_low(matrix):
    high = matrix.astype(jnp.bfloat16)
    low = (matrix - high.astype(np.float64)).astype(jnp.bfloat16)
    return high, low


def transforms():
    row = np.arange(POINTS)
    angle = 2 * np.pi * np.outer(np.arange(HALF), row) / POINTS
    sine = -np.sin(angle)
    sine[0] = (-1.0) ** row
    forward = np.concatenate([np.cos(angle), sine], axis=0)
    back_cos = np.cos(angle[:, HALF:]).T * (2 / POINTS)
    back_cos[:, 0] = 1 / POINTS
    back_sine = -np.sin(angle[:, HALF:]).T * (2 / POINTS)
    back_sine[:, 0] = (-1.0) ** row[HALF:] / POINTS
    back = np.concatenate([back_cos, back_sine], axis=1)
    return split_high_low(forward) + split_high_low(back)


def dot(a, b):
    return lax.dot_general(a, b, (((1,), (0,)), ((), ())), preferred_element_type=F32)


def dot_nt(a, b):
    return lax.dot_general(a, b, (((1,), (1,)), ((), ())), preferred_element_type=F32)


def mixer_kernel(
    owner_ref, listed_ref, short_ref, long_ref, down_ref, up_ref,
    q_hbm, k_hbm, v_hbm, fwd_hi_hbm, fwd_lo_hbm, back_hi_hbm, back_lo_hbm,
    out_ref,
    q_ref, k_ref, v_ref, fwd_hi, fwd_lo, back_hi, back_lo,
    own_list, lists, slab_lists, bank_down, bank_up, send_x, recv_x, part_b, sum_b, part_a, sum_a, fin,
    own_short, short_all, first_long, long_all, even_taps, odd_taps, own_tail, tails, halo,
    gate_hi, filt_re, filt_im, filt_re2, q_short, mixed,
    load_sem, list_sem, tail_sem, halo_send, halo_recv, f_send, f_recv, a_send, a_recv,
):
    group = lax.axis_index("group")
    ctx = lax.axis_index("ctx")
    x, core = group // 2, group % 2
    y, z = ctx // 16, ctx % 16
    z_low, z_high = z % 4, z // 4
    has_before = ctx > 0

    def at_y(d):
        return (group, ((y + d) % 4) * 16 + z)

    def at_z(d):
        return (group, y * 16 + (z + d + 16) % 16)

    def at_x(d):
        return (((x + d) % 4) * 2 + core, ctx)

    def at_group(d):
        return ((group + d) % 8, ctx)

    after = (group, (ctx + 1) % 64)
    before = (group, (ctx + 63) % 64)

    barrier = pltpu.get_barrier_semaphore()
    peers = [at_y(d) for d in (1, 2, 3)] + [at_group(d) for d in range(1, 8)]
    peers += [at_z(d) for d in range(1, 16)] + [after, before]
    for peer in peers:
        pl.semaphore_signal(barrier, inc=1, device_id=peer, device_id_type=MESH)

    sources = (q_hbm, k_hbm, v_hbm, fwd_hi_hbm, fwd_lo_hbm, back_hi_hbm, back_lo_hbm)
    places = (q_ref, k_ref, v_ref, fwd_hi, fwd_lo, back_hi, back_lo)
    loads = [
        pltpu.make_async_copy(src, dst, load_sem.at[i])
        for i, (src, dst) in enumerate(zip(sources, places))
    ]
    for load in loads:
        load.start()

    own_list[...] = jnp.broadcast_to(
        jnp.concatenate([listed_ref[...], jnp.zeros((1, 120), jnp.int32)], axis=1), (8, 128)
    )
    taps = [short_ref[n // 3, n % 3:n % 3 + 1, :] for n in range(9)]
    taps += [jnp.zeros((1, 64), F32)] * 7
    for r in range(8):
        own_short[r:r + 1, :] = jnp.concatenate(taps[2 * r:2 * r + 2], axis=1)
    short_all[ctx] = own_short[...]
    tail_row = lax.broadcasted_iota(jnp.int32, (16, CHUNK), 0)

    def columns(c):
        return pl.ds(pl.multiple_of(c * CHUNK, CHUNK), CHUNK)

    def pack_tail(c, carry):
        at = columns(c)
        last = [ref[ROWS - 16:, at].astype(F32) for ref in (q_ref, k_ref, v_ref)]
        packed = jnp.where(tail_row < 6, pltpu.roll(last[2], 6, 0), 0.0)
        packed = jnp.where(tail_row < 4, pltpu.roll(last[1], 4, 0), packed)
        packed = jnp.where(tail_row < 2, pltpu.roll(last[0], 2, 0), packed)
        own_tail[:, at] = packed.astype(BF)
        return carry

    first_long[y] = long_ref[...]
    bank = (bank_down, bank_up)
    bank_down[y] = down_ref[...]
    bank_up[y] = up_ref[...]
    for load in loads[:3]:
        load.wait()
    lax.fori_loop(0, CHUNKS, pack_tail, 0)
    pl.semaphore_wait(barrier, len(peers))

    pending = []
    used = {"f": 0, "a": 0}

    def send(kind, src, dst, peer):
        at = used[kind]
        used[kind] += 1
        sems = (f_send, f_recv) if kind == "f" else (a_send, a_recv)
        copy = pltpu.make_async_remote_copy(
            src, dst, sems[0].at[at], sems[1].at[at], device_id=peer, device_id_type=MESH
        )
        copy.start()
        pending.append(copy)
        return copy

    def arrived(copies):
        for copy in copies:
            copy.wait_recv()

    bank_y = [
        [send("a", (down_ref, up_ref)[m], bank[m].at[y], at_y(d)) for d in (1, 2, 3)]
        for m in range(2)
    ]
    listed_all = [send("f", own_list, lists.at[group], at_group(d)) for d in range(1, 8)]
    lists[group] = own_list[...]
    arrived(listed_all)
    to_scalar = pltpu.make_async_copy(lists, slab_lists, list_sem.at[0])
    to_scalar.start()
    to_scalar.wait()

    bank_x = []
    for m in range(2):
        arrived(bank_y[m])
        copies = []
        for d in range(8):
            slab = (group + d) % 8
            for e in range(2):
                slot = owner_ref[slab_lists[slab, 0, y + 4 * e]]
                keep = ((slot // 4) % 16 == z).astype(F32)
                one = (bank[m][slot // 64, slot % 4].astype(F32) * keep).astype(BF)
                if d == 0:
                    recv_x[m, e, group // 4, group % 4] = one
                else:
                    send_x[m, d - 1, e] = one
            if d:
                copies.append(send(
                    "a", send_x.at[m, d - 1], recv_x.at[m, :, group // 4, group % 4], at_group(d)
                ))
        bank_x.append(copies)

    short_z = [send("f", own_short, short_all.at[ctx], at_z(d)) for d in range(1, 16)]
    long_y = [send("f", long_ref, first_long.at[y], at_y(d)) for d in (1, 2, 3)]

    def send_near(m):
        arrived(bank_x[m])
        copies = []
        for j, d in enumerate((1, -1, -2)):
            to = (z + d + 16) % 4
            copies.append(send("a", recv_x.at[m, to // 2, to % 2], part_b.at[m, j], at_z(d)))
        return copies


    bank_near = [send_near(0)]
    bank_near.append(send_near(1))
    tail_copy = pltpu.make_async_remote_copy(
        own_tail, tails, tail_sem.at[0], tail_sem.at[1], device_id=after, device_id_type=MESH
    )
    tail_copy.start()
    arrived(short_z)
    row16 = pl.ds(y * 16, 16)
    short_y = [send("f", short_all.at[row16], short_all.at[row16], at_y(d)) for d in (1, 2, 3)]

    arrived(long_y)
    mine = x * 16 + z_low * 4 + z_high
    long_far = [send("f", first_long.at[x], long_all.at[mine], at_z(d)) for d in (4, 8, -4)]
    long_all[mine] = first_long[x]

    bank_far = []
    for m in range(2):
        arrived(bank_near[m])
        for c in range(4):
            sum_b[m, c] = (
                recv_x[m, z_low // 2, z_low % 2, c].astype(F32) + part_b[m, 0, c].astype(F32)
                + part_b[m, 1, c].astype(F32) + part_b[m, 2, c].astype(F32)
            ).astype(BF)
        copies = []
        for j in (1, 2, 3):
            cols = pl.ds(pl.multiple_of(((z_high + j) % 4) * 128, 128), 128)
            copies.append(send("a", sum_b.at[m, :, :, cols], part_a.at[m, j - 1], at_z(4 * j)))
        bank_far.append(copies)

    tail_copy.wait_recv()
    arrived(short_y)
    lane = lax.broadcasted_iota(jnp.int32, (8, 128), 1)

    def unpack(i, carry):
        one, two = short_all[2 * i], short_all[2 * i + 1]
        at = pl.ds(pl.multiple_of(i * 128, 128), 128)
        even_taps[:, at] = jnp.where(lane < 64, one, pltpu.roll(two, 64, 1))
        odd_taps[:, at] = jnp.where(lane < 64, pltpu.roll(one, 64, 1), two)
        return carry

    lax.fori_loop(0, WIDTH // 128, unpack, 0)
    row = lax.broadcasted_iota(jnp.int32, (ROWS, CHUNK), 0)

    def short_filter(ref, stream, at):
        signal = ref[:, at].astype(F32)
        edge = jnp.where(has_before, tails[:, at].astype(F32), 0.0)
        older, newer = edge[2 * stream:2 * stream + 1], edge[2 * stream + 1:2 * stream + 2]
        back1 = jnp.where(row == 0, newer, pltpu.roll(signal, 1, 0))
        back2 = jnp.where(row == 0, older, jnp.where(row == 1, newer, pltpu.roll(signal, 2, 0)))
        total = None
        for j, shifted in enumerate((signal, back1, back2)):
            n = 3 * stream + j
            taps = (even_taps if n % 2 == 0 else odd_taps)[n // 2:n // 2 + 1, at]
            total = taps * shifted if total is None else total + taps * shifted
        return total

    def halo_copy(c):
        at = columns(c)
        return pltpu.make_async_remote_copy(
            gate_hi.at[:, at], halo.at[:, at], halo_send.at[c], halo_recv.at[c],
            device_id=after, device_id_type=MESH,
        )

    def gate(c, carry):
        at = columns(c)
        gated = short_filter(k_ref, 1, at) * short_filter(v_ref, 2, at)
        gate_hi[:, at] = gated.astype(BF)
        return carry

    def send_halo(c, carry):
        halo_copy(c).start()
        return carry


    lax.fori_loop(0, CHUNKS, gate, 0)
    arrived(long_far)
    quad = pl.ds(x * 16 + z_low * 4, 4)
    long_near = [send("f", long_all.at[quad], long_all.at[quad], at_z(d)) for d in (1, -1, -2)]

    own = pl.ds(pl.multiple_of(z_high * 128, 128), 128)
    to_far = []
    for m in range(2):
        arrived(bank_far[m])
        for c in range(4):
            total = (
                sum_b[m, c, :, own].astype(F32) + part_a[m, 0, c].astype(F32)
                + part_a[m, 1, c].astype(F32) + part_a[m, 2, c].astype(F32)
            ).astype(BF)
            sum_a[m, c] = total
            fin[m, y, z_low // 2, z_low % 2, c, :, own] = total
        target = fin.at[m, y, z_low // 2, z_low % 2, :, :, own]
        to_far.append([send("a", sum_a.at[m], target, at_z(4 * j)) for j in (1, 2, 3)])

    for load in loads[3:]:
        load.wait()
    def own_rows(c, carry):
        at = columns(c)
        q_short[:, at] = short_filter(q_ref, 0, at)
        return carry

    lax.fori_loop(0, CHUNKS, own_rows, 0)

    arrived(long_near)
    row16x = pl.ds(x * 16, 16)
    long_x = [send("f", long_all.at[row16x], long_all.at[row16x], at_x(d)) for d in (1, 2, 3)]

    def block_of(m, from_y, near_z):
        k = (near_z + 16) % 4
        return fin.at[m, (from_y + 4) % 4, k // 2, k % 2]

    def to_near(m):
        block = block_of(m, y, z)
        return [send("a", block, block, at_z(d)) for d in (1, -1, -2)]

    def to_y(m, near_z):
        block = block_of(m, y, near_z)
        return [send("a", block, block, at_y(d)) for d in (1, 3)]

    near_in, y_in = [], []
    for m in range(2):
        arrived(to_far[m])
        near_in.append(to_near(m))
    y_in.append([to_y(0, z), to_y(1, z)])
    lax.fori_loop(0, CHUNKS, send_halo, 0)
    def mix(c, carry):
        at = columns(c)
        halo_copy(c).wait_recv()
        old = jnp.where(has_before, halo[:, at].astype(F32), 0.0).astype(BF)
        total = dot(fwd_hi[...], jnp.concatenate([old, gate_hi[:, at]], axis=0))
        re, im = total[:HALF], total[HALF:]
        f_im = filt_im[:, at]
        prod_re = re * filt_re[:, at] - im * f_im
        prod_im = re * f_im + im * filt_re2[:, at]
        re_hi, im_hi = prod_re.astype(BF), prod_im.astype(BF)
        re_lo = (prod_re - re_hi.astype(F32)).astype(BF)
        im_lo = (prod_im - im_hi.astype(F32)).astype(BF)
        high = jnp.concatenate([re_hi, im_hi], axis=0)
        low = jnp.concatenate([re_lo, im_lo], axis=0)
        long_conv = dot(back_hi[...], high) + dot(back_lo[...], high) + dot(back_hi[...], low)
        mixed[:, at] = (q_short[:, at] * long_conv).astype(BF)
        return carry

    for j, d in enumerate((-1, 1, 2)):
        pair = []
        for m in range(2):
            arrived([near_in[m][j]])
            pair.append(to_y(m, z + d))
        y_in.append(pair)

    arrived(long_x)

    def filters(c, carry):
        at = columns(c)
        blocks = []
        for i in range(8):
            from_z = 8 * (c % 2) + i
            blocks.append(long_all[(c // 2) * 16 + (from_z % 4) * 4 + from_z // 4])
        taps = jnp.concatenate(blocks, axis=0)
        filt = dot_nt(fwd_hi[:, :HALF], taps) + dot_nt(fwd_lo[:, :HALF], taps)
        re, im = filt[:HALF], filt[HALF:]
        filt_re[:, at] = re
        filt_im[:, at] = jnp.where(row == 0, 0.0, im)
        filt_re2[:, at] = jnp.where(row == 0, im, re)
        return carry

    lax.fori_loop(0, CHUNKS, filters, 0)

    def forward(j, d):
        (down_right, _), (_, up_left) = y_in[j]
        arrived([down_right])
        block = block_of(0, y - 1, z + d)
        down_two.append(send("a", block, block, at_y(1)))
        arrived([up_left])
        block = block_of(1, y + 1, z + d)
        up_two.append(send("a", block, block, at_y(3)))

    down_two, up_two = [], []
    for j, d in enumerate((0, -1, 1, 2)):
        forward(j, d)
        lax.fori_loop(j, j + 1, mix, 0)
    lax.fori_loop(4, CHUNKS, mix, 0)
    down_in = [pair[0][1] for pair in y_in] + down_two
    up_in = [pair[1][0] for pair in y_in] + up_two

    def maps(m, c):
        return fin[m, :, :, c // 4, c % 4].reshape(ROWS, CHUNK)

    arrived(down_in)

    def down(c, total):
        return total + dot_nt(mixed[:, columns(c)], maps(0, c))

    low_rank = lax.fori_loop(0, CHUNKS, down, jnp.zeros((ROWS, ROWS), F32)).astype(BF)
    arrived(up_in)

    def up(c, carry):
        at = columns(c)
        out_ref[:, at] = (mixed[:, at].astype(F32) + dot(low_rank, maps(1, c))).astype(BF)
        return carry

    lax.fori_loop(0, CHUNKS, up, 0)

    tail_copy.wait_send()
    for copy in pending:
        copy.wait_send()

    def drain(c, carry):
        halo_copy(c).wait_send()
        return carry

    lax.fori_loop(0, CHUNKS, drain, 0)


def on_device(
    projected_queries,
    projected_keys,
    projected_values,
    short_filter_taps,
    long_filter_taps,
    adapter_down_weight,
    adapter_up_weight,
    slab_adapter_index,
    adapter_owner_slot,
):
    constants = [jnp.asarray(part) for part in transforms()]
    vmem = pl.BlockSpec(memory_space=pltpu.VMEM)
    return pl.pallas_call(
        mixer_kernel,
        out_shape=jax.ShapeDtypeStruct((ROWS, WIDTH), BF),
        in_specs=(
            [pl.BlockSpec(memory_space=pltpu.SMEM)] + [vmem] * 5
            + [pl.BlockSpec(memory_space=pl.ANY)] * 7
        ),
        out_specs=vmem,
        scratch_shapes=[
            pltpu.VMEM((ROWS, WIDTH), BF),
            pltpu.VMEM((ROWS, WIDTH), BF),
            pltpu.VMEM((ROWS, WIDTH), BF),
            pltpu.VMEM((POINTS, POINTS), BF),
            pltpu.VMEM((POINTS, POINTS), BF),
            pltpu.VMEM((HALF, POINTS), BF),
            pltpu.VMEM((HALF, POINTS), BF),
            pltpu.VMEM((8, 128), jnp.int32),
            pltpu.VMEM((8, 8, 128), jnp.int32),
            pltpu.SMEM((8, 8, 128), jnp.int32),
            pltpu.VMEM((4, 4, 16, CHUNK), BF),
            pltpu.VMEM((4, 4, 16, CHUNK), BF),
            pltpu.VMEM((2, 7, 2, 16, CHUNK), BF),
            pltpu.VMEM((2, 2, 2, 4, 16, CHUNK), BF),
            pltpu.VMEM((2, 3, 4, 16, CHUNK), BF),
            pltpu.VMEM((2, 4, 16, CHUNK), BF),
            pltpu.VMEM((2, 3, 4, 16, 128), BF),
            pltpu.VMEM((2, 4, 16, 128), BF),
            pltpu.VMEM((2, 4, 2, 2, 4, 16, CHUNK), BF),
            pltpu.VMEM((8, 128), F32),
            pltpu.VMEM((64, 8, 128), F32),
            pltpu.VMEM((4, 64, 128), BF),
            pltpu.VMEM((64, 64, 128), BF),
            pltpu.VMEM((8, WIDTH), F32),
            pltpu.VMEM((8, WIDTH), F32),
            pltpu.VMEM((16, WIDTH), BF),
            pltpu.VMEM((16, WIDTH), BF),
            pltpu.VMEM((ROWS, WIDTH), BF),
            pltpu.VMEM((ROWS, WIDTH), BF),
            pltpu.VMEM((HALF, WIDTH), F32),
            pltpu.VMEM((HALF, WIDTH), F32),
            pltpu.VMEM((HALF, WIDTH), F32),
            pltpu.VMEM((ROWS, WIDTH), F32),
            pltpu.VMEM((ROWS, WIDTH), BF),
            pltpu.SemaphoreType.DMA((7,)),
            pltpu.SemaphoreType.DMA((1,)),
            pltpu.SemaphoreType.DMA((2,)),
            pltpu.SemaphoreType.DMA((CHUNKS,)),
            pltpu.SemaphoreType.DMA((CHUNKS,)),
            pltpu.SemaphoreType.DMA((37,)),
            pltpu.SemaphoreType.DMA((37,)),
            pltpu.SemaphoreType.DMA((68,)),
            pltpu.SemaphoreType.DMA((68,)),
        ],
        compiler_params=pltpu.CompilerParams(
            collective_id=0, has_side_effects=True, vmem_limit_bytes=56 * 1024 * 1024
        ),
        cost_estimate=pl.CostEstimate(
            flops=3_000_000_000, bytes_accessed=8_000_000, transcendentals=0
        ),
    )(
        adapter_owner_slot, slab_adapter_index, short_filter_taps, long_filter_taps.T,
        adapter_down_weight, adapter_up_weight, projected_queries, projected_keys,
        projected_values, *constants,
    )


def solution(mesh):
    in_specs = (
        P(("group", "ctx"), None),
        P(("group", "ctx"), None),
        P(("group", "ctx"), None),
        P(None, None, "ctx"),
        P(None, "ctx"),
        P("ctx", None, "group"),
        P("ctx", None, "group"),
        P("group", None),
        P(),
    )
    out_specs = P(("group", "ctx"), None)
    return jax.shard_map(
        on_device, mesh=mesh, in_specs=in_specs, out_specs=out_specs, check_vma=False
    )
```

```python
import jax
import jax.numpy as jnp
import numpy as np
from jax import lax
from jax.experimental import pallas as pl
from jax.experimental.pallas import tpu as pltpu
from jax.sharding import PartitionSpec as P

MESH = pl.DeviceIdType.MESH
BF = jnp.bfloat16
F32 = jnp.float32
ROWS = 128
WIDTH = 4096
CHUNK = 512
CHUNKS = WIDTH // CHUNK
POINTS = 256
HALF = POINTS // 2


def split_high_low(matrix):
    high = matrix.astype(jnp.bfloat16)
    low = (matrix - high.astype(np.float64)).astype(jnp.bfloat16)
    return high, low


def transforms():
    row = np.arange(POINTS)
    angle = 2 * np.pi * np.outer(np.arange(HALF), row) / POINTS
    sine = -np.sin(angle)
    sine[0] = (-1.0) ** row
    forward = np.concatenate([np.cos(angle), sine], axis=0)
    back_cos = np.cos(angle[:, HALF:]).T * (2 / POINTS)
    back_cos[:, 0] = 1 / POINTS
    back_sine = -np.sin(angle[:, HALF:]).T * (2 / POINTS)
    back_sine[:, 0] = (-1.0) ** row[HALF:] / POINTS
    back = np.concatenate([back_cos, back_sine], axis=1)
    return split_high_low(forward) + split_high_low(back)


def dot(a, b):
    return lax.dot_general(a, b, (((1,), (0,)), ((), ())), preferred_element_type=F32)


def dot_nt(a, b):
    return lax.dot_general(a, b, (((1,), (1,)), ((), ())), preferred_element_type=F32)


def mixer_kernel(
    owner_ref, listed_ref, short_ref, long_ref, down_ref, up_ref,
    q_hbm, k_hbm, v_hbm, fwd_hi_hbm, fwd_lo_hbm, back_hi_hbm, back_lo_hbm,
    out_ref,
    q_ref, k_ref, v_ref, fwd_hi, fwd_lo, back_hi, back_lo,
    own_list, lists, slab_lists, bank_down, bank_up, send_x, recv_x, part_b, sum_b, part_a, sum_a, fin,
    own_short, short_all, first_long, long_all, even_taps, odd_taps, own_tail, tails, halo,
    gate_hi, gate_lo, spectrum, filt_re, filt_im, filt_re2, q_short, mixed,
    load_sem, list_sem, tail_sem, halo_send, halo_recv, f_send, f_recv, a_send, a_recv,
):
    group = lax.axis_index("group")
    ctx = lax.axis_index("ctx")
    x, core = group // 2, group % 2
    y, z = ctx // 16, ctx % 16
    z_low, z_high = z % 4, z // 4
    has_before = ctx > 0

    def at_y(d):
        return (group, ((y + d) % 4) * 16 + z)

    def at_z(d):
        return (group, y * 16 + (z + d + 16) % 16)

    def at_x(d):
        return (((x + d) % 4) * 2 + core, ctx)

    def at_group(d):
        return ((group + d) % 8, ctx)

    after = (group, (ctx + 1) % 64)
    before = (group, (ctx + 63) % 64)

    barrier = pltpu.get_barrier_semaphore()
    peers = [at_y(d) for d in (1, 2, 3)] + [at_group(d) for d in range(1, 8)]
    peers += [at_z(d) for d in range(1, 16)] + [after, before]
    for peer in peers:
        pl.semaphore_signal(barrier, inc=1, device_id=peer, device_id_type=MESH)

    sources = (q_hbm, k_hbm, v_hbm, fwd_hi_hbm, fwd_lo_hbm, back_hi_hbm, back_lo_hbm)
    places = (q_ref, k_ref, v_ref, fwd_hi, fwd_lo, back_hi, back_lo)
    loads = [
        pltpu.make_async_copy(src, dst, load_sem.at[i])
        for i, (src, dst) in enumerate(zip(sources, places))
    ]
    for load in loads:
        load.start()

    own_list[...] = jnp.broadcast_to(
        jnp.concatenate([listed_ref[...], jnp.zeros((1, 120), jnp.int32)], axis=1), (8, 128)
    )
    taps = [short_ref[n // 3, n % 3:n % 3 + 1, :] for n in range(9)]
    taps += [jnp.zeros((1, 64), F32)] * 7
    for r in range(8):
        own_short[r:r + 1, :] = jnp.concatenate(taps[2 * r:2 * r + 2], axis=1)
    short_all[ctx] = own_short[...]
    tail_row = lax.broadcasted_iota(jnp.int32, (16, CHUNK), 0)

    def columns(c):
        return pl.ds(pl.multiple_of(c * CHUNK, CHUNK), CHUNK)

    def pack_tail(c, carry):
        at = columns(c)
        last = [ref[ROWS - 16:, at].astype(F32) for ref in (q_ref, k_ref, v_ref)]
        packed = jnp.where(tail_row < 6, pltpu.roll(last[2], 6, 0), 0.0)
        packed = jnp.where(tail_row < 4, pltpu.roll(last[1], 4, 0), packed)
        packed = jnp.where(tail_row < 2, pltpu.roll(last[0], 2, 0), packed)
        own_tail[:, at] = packed.astype(BF)
        return carry

    first_long[y] = long_ref[...]
    bank = (bank_down, bank_up)
    bank_down[y] = down_ref[...]
    bank_up[y] = up_ref[...]
    pl.semaphore_wait(barrier, len(peers))

    pending = []
    used = {"f": 0, "a": 0}

    def send(kind, src, dst, peer):
        at = used[kind]
        used[kind] += 1
        sems = (f_send, f_recv) if kind == "f" else (a_send, a_recv)
        copy = pltpu.make_async_remote_copy(
            src, dst, sems[0].at[at], sems[1].at[at], device_id=peer, device_id_type=MESH
        )
        copy.start()
        pending.append(copy)
        return copy

    def arrived(copies):
        for copy in copies:
            copy.wait_recv()

    bank_y = [
        [send("a", (down_ref, up_ref)[m], bank[m].at[y], at_y(d)) for d in (1, 2, 3)]
        for m in range(2)
    ]
    short_z = [send("f", own_short, short_all.at[ctx], at_z(d)) for d in range(1, 16)]
    listed_all = [send("f", own_list, lists.at[group], at_group(d)) for d in range(1, 8)]
    lists[group] = own_list[...]
    long_y = [send("f", long_ref, first_long.at[y], at_y(d)) for d in (1, 2, 3)]

    arrived(listed_all)
    to_scalar = pltpu.make_async_copy(lists, slab_lists, list_sem.at[0])
    to_scalar.start()
    to_scalar.wait()

    bank_x = []
    for m in range(2):
        arrived(bank_y[m])
        copies = []
        for d in range(8):
            slab = (group + d) % 8
            for e in range(2):
                slot = owner_ref[slab_lists[slab, 0, y + 4 * e]]
                keep = ((slot // 4) % 16 == z).astype(F32)
                one = (bank[m][slot // 64, slot % 4].astype(F32) * keep).astype(BF)
                if d == 0:
                    recv_x[m, e, group // 4, group % 4] = one
                else:
                    send_x[m, d - 1, e] = one
            if d:
                copies.append(send(
                    "a", send_x.at[m, d - 1], recv_x.at[m, :, group // 4, group % 4], at_group(d)
                ))
        bank_x.append(copies)

    for load in loads[:3]:
        load.wait()
    lax.fori_loop(0, CHUNKS, pack_tail, 0)
    tail_copy = pltpu.make_async_remote_copy(
        own_tail, tails, tail_sem.at[0], tail_sem.at[1], device_id=after, device_id_type=MESH
    )
    tail_copy.start()
    arrived(long_y)
    mine = x * 16 + z_low * 4 + z_high
    long_far = [send("f", first_long.at[x], long_all.at[mine], at_z(d)) for d in (4, 8, -4)]
    long_all[mine] = first_long[x]

    def send_near(m):
        arrived(bank_x[m])
        copies = []
        for j, d in enumerate((1, -1, -2)):
            to = (z + d + 16) % 4
            copies.append(send("a", recv_x.at[m, to // 2, to % 2], part_b.at[m, j], at_z(d)))
        return copies


    bank_near = [send_near(0)]
    arrived(short_z)
    row16 = pl.ds(y * 16, 16)
    short_y = [send("f", short_all.at[row16], short_all.at[row16], at_y(d)) for d in (1, 2, 3)]

    bank_near.append(send_near(1))
    tail_copy.wait_recv()
    arrived(short_y)
    lane = lax.broadcasted_iota(jnp.int32, (8, 128), 1)

    def unpack(i, carry):
        one, two = short_all[2 * i], short_all[2 * i + 1]
        at = pl.ds(pl.multiple_of(i * 128, 128), 128)
        even_taps[:, at] = jnp.where(lane < 64, one, pltpu.roll(two, 64, 1))
        odd_taps[:, at] = jnp.where(lane < 64, pltpu.roll(one, 64, 1), two)
        return carry

    lax.fori_loop(0, WIDTH // 128, unpack, 0)
    row = lax.broadcasted_iota(jnp.int32, (ROWS, CHUNK), 0)

    def short_filter(ref, stream, at):
        signal = ref[:, at].astype(F32)
        edge = jnp.where(has_before, tails[:, at].astype(F32), 0.0)
        older, newer = edge[2 * stream:2 * stream + 1], edge[2 * stream + 1:2 * stream + 2]
        back1 = jnp.where(row == 0, newer, pltpu.roll(signal, 1, 0))
        back2 = jnp.where(row == 0, older, jnp.where(row == 1, newer, pltpu.roll(signal, 2, 0)))
        total = None
        for j, shifted in enumerate((signal, back1, back2)):
            n = 3 * stream + j
            taps = (even_taps if n % 2 == 0 else odd_taps)[n // 2:n // 2 + 1, at]
            total = taps * shifted if total is None else total + taps * shifted
        return total

    def halo_copy(c):
        at = columns(c)
        return pltpu.make_async_remote_copy(
            gate_hi.at[:, at], halo.at[:, at], halo_send.at[c], halo_recv.at[c],
            device_id=after, device_id_type=MESH,
        )

    def gate(c, carry):
        at = columns(c)
        gated = short_filter(k_ref, 1, at) * short_filter(v_ref, 2, at)
        high = gated.astype(BF)
        gate_hi[:, at] = high
        gate_lo[:, at] = (gated - high.astype(F32)).astype(BF)
        return carry

    def send_halo(c, carry):
        halo_copy(c).start()
        return carry


    lax.fori_loop(0, 2, gate, 0)
    lax.fori_loop(0, 2, send_halo, 0)
    bank_far = []
    for m in range(2):
        arrived(bank_near[m])
        for c in range(4):
            sum_b[m, c] = (
                recv_x[m, z_low // 2, z_low % 2, c].astype(F32) + part_b[m, 0, c].astype(F32)
                + part_b[m, 1, c].astype(F32) + part_b[m, 2, c].astype(F32)
            ).astype(BF)
        copies = []
        for j in (1, 2, 3):
            cols = pl.ds(pl.multiple_of(((z_high + j) % 4) * 128, 128), 128)
            copies.append(send("a", sum_b.at[m, :, :, cols], part_a.at[m, j - 1], at_z(4 * j)))
        bank_far.append(copies)

    lax.fori_loop(2, CHUNKS, gate, 0)
    lax.fori_loop(2, 5, send_halo, 0)
    arrived(long_far)
    quad = pl.ds(x * 16 + z_low * 4, 4)
    long_near = [send("f", long_all.at[quad], long_all.at[quad], at_z(d)) for d in (1, -1, -2)]

    for load in loads[3:]:
        load.wait()
    def own_rows(c, carry):
        at = columns(c)
        q_short[:, at] = short_filter(q_ref, 0, at)
        high, low = gate_hi[:, at], gate_lo[:, at]
        spectrum[:, at] = (
            dot(fwd_hi[:, HALF:], high) + dot(fwd_lo[:, HALF:], high) + dot(fwd_hi[:, HALF:], low)
        )
        return carry

    lax.fori_loop(0, CHUNKS, own_rows, 0)

    own = pl.ds(pl.multiple_of(z_high * 128, 128), 128)
    to_far = []
    for m in range(2):
        arrived(bank_far[m])
        for c in range(4):
            total = (
                sum_b[m, c, :, own].astype(F32) + part_a[m, 0, c].astype(F32)
                + part_a[m, 1, c].astype(F32) + part_a[m, 2, c].astype(F32)
            ).astype(BF)
            sum_a[m, c] = total
            fin[m, y, z_low // 2, z_low % 2, c, :, own] = total
        target = fin.at[m, y, z_low // 2, z_low % 2, :, :, own]
        to_far.append([send("a", sum_a.at[m], target, at_z(4 * j)) for j in (1, 2, 3)])

    lax.fori_loop(5, CHUNKS, send_halo, 0)
    arrived(long_near)
    row16x = pl.ds(x * 16, 16)
    long_x = [send("f", long_all.at[row16x], long_all.at[row16x], at_x(d)) for d in (1, 2, 3)]

    to_near, to_y = [], [[], []]
    for m in range(2):
        arrived(to_far[m])
        block = fin.at[m, y, z_low // 2, z_low % 2]
        to_near.append([send("a", block, block, at_z(d)) for d in (1, -1, -2)])
        to_y[m] += [send("a", block, block, at_y(d)) for d in (1, 2, 3)]

    arrived(long_x)

    def filters(c, carry):
        at = columns(c)
        blocks = []
        for i in range(8):
            from_z = 8 * (c % 2) + i
            blocks.append(long_all[(c // 2) * 16 + (from_z % 4) * 4 + from_z // 4])
        taps = jnp.concatenate(blocks, axis=0)
        filt = dot_nt(fwd_hi[:, :HALF], taps) + dot_nt(fwd_lo[:, :HALF], taps)
        re, im = filt[:HALF], filt[HALF:]
        filt_re[:, at] = re
        filt_im[:, at] = jnp.where(row == 0, 0.0, im)
        filt_re2[:, at] = jnp.where(row == 0, im, re)
        return carry

    lax.fori_loop(0, CHUNKS, filters, 0)

    def pass_on(m):
        for copy, d in zip(to_near[m], (-1, 1, 2)):
            arrived([copy])
            k = (z + d + 16) % 4
            block = fin.at[m, y, k // 2, k % 2]
            to_y[m].extend([send("a", block, block, at_y(e)) for e in (1, 2, 3)])

    pass_on(0)
    pass_on(1)
    def mix(c, carry):
        at = columns(c)
        halo_copy(c).wait_recv()
        old = jnp.where(has_before, halo[:, at].astype(F32), 0.0).astype(BF)
        total = spectrum[:, at] + dot(fwd_hi[:, :HALF], old) + dot(fwd_lo[:, :HALF], old)
        re, im = total[:HALF], total[HALF:]
        f_im = filt_im[:, at]
        prod_re = re * filt_re[:, at] - im * f_im
        prod_im = re * f_im + im * filt_re2[:, at]
        re_hi, im_hi = prod_re.astype(BF), prod_im.astype(BF)
        re_lo = (prod_re - re_hi.astype(F32)).astype(BF)
        im_lo = (prod_im - im_hi.astype(F32)).astype(BF)
        high = jnp.concatenate([re_hi, im_hi], axis=0)
        low = jnp.concatenate([re_lo, im_lo], axis=0)
        long_conv = dot(back_hi[...], high) + dot(back_lo[...], high) + dot(back_hi[...], low)
        mixed[:, at] = (q_short[:, at] * long_conv).astype(BF)
        return carry

    lax.fori_loop(0, CHUNKS, mix, 0)

    def maps(m, c):
        return fin[m, :, :, c // 4, c % 4].reshape(ROWS, CHUNK)

    arrived(to_y[0])

    def down(c, total):
        return total + dot_nt(mixed[:, columns(c)], maps(0, c))

    low_rank = lax.fori_loop(0, CHUNKS, down, jnp.zeros((ROWS, ROWS), F32)).astype(BF)
    arrived(to_y[1])

    def up(c, carry):
        at = columns(c)
        out_ref[:, at] = (mixed[:, at].astype(F32) + dot(low_rank, maps(1, c))).astype(BF)
        return carry

    lax.fori_loop(0, CHUNKS, up, 0)

    tail_copy.wait_send()
    for copy in pending:
        copy.wait_send()

    def drain(c, carry):
        halo_copy(c).wait_send()
        return carry

    lax.fori_loop(0, CHUNKS, drain, 0)


def on_device(
    projected_queries,
    projected_keys,
    projected_values,
    short_filter_taps,
    long_filter_taps,
    adapter_down_weight,
    adapter_up_weight,
    slab_adapter_index,
    adapter_owner_slot,
):
    constants = [jnp.asarray(part) for part in transforms()]
    vmem = pl.BlockSpec(memory_space=pltpu.VMEM)
    return pl.pallas_call(
        mixer_kernel,
        out_shape=jax.ShapeDtypeStruct((ROWS, WIDTH), BF),
        in_specs=(
            [pl.BlockSpec(memory_space=pltpu.SMEM)] + [vmem] * 5
            + [pl.BlockSpec(memory_space=pl.ANY)] * 7
        ),
        out_specs=vmem,
        scratch_shapes=[
            pltpu.VMEM((ROWS, WIDTH), BF),
            pltpu.VMEM((ROWS, WIDTH), BF),
            pltpu.VMEM((ROWS, WIDTH), BF),
            pltpu.VMEM((POINTS, POINTS), BF),
            pltpu.VMEM((POINTS, POINTS), BF),
            pltpu.VMEM((HALF, POINTS), BF),
            pltpu.VMEM((HALF, POINTS), BF),
            pltpu.VMEM((8, 128), jnp.int32),
            pltpu.VMEM((8, 8, 128), jnp.int32),
            pltpu.SMEM((8, 8, 128), jnp.int32),
            pltpu.VMEM((4, 4, 16, CHUNK), BF),
            pltpu.VMEM((4, 4, 16, CHUNK), BF),
            pltpu.VMEM((2, 7, 2, 16, CHUNK), BF),
            pltpu.VMEM((2, 2, 2, 4, 16, CHUNK), BF),
            pltpu.VMEM((2, 3, 4, 16, CHUNK), BF),
            pltpu.VMEM((2, 4, 16, CHUNK), BF),
            pltpu.VMEM((2, 3, 4, 16, 128), BF),
            pltpu.VMEM((2, 4, 16, 128), BF),
            pltpu.VMEM((2, 4, 2, 2, 4, 16, CHUNK), BF),
            pltpu.VMEM((8, 128), F32),
            pltpu.VMEM((64, 8, 128), F32),
            pltpu.VMEM((4, 64, 128), BF),
            pltpu.VMEM((64, 64, 128), BF),
            pltpu.VMEM((8, WIDTH), F32),
            pltpu.VMEM((8, WIDTH), F32),
            pltpu.VMEM((16, WIDTH), BF),
            pltpu.VMEM((16, WIDTH), BF),
            pltpu.VMEM((ROWS, WIDTH), BF),
            pltpu.VMEM((ROWS, WIDTH), BF),
            pltpu.VMEM((ROWS, WIDTH), BF),
            pltpu.VMEM((POINTS, WIDTH), F32),
            pltpu.VMEM((HALF, WIDTH), F32),
            pltpu.VMEM((HALF, WIDTH), F32),
            pltpu.VMEM((HALF, WIDTH), F32),
            pltpu.VMEM((ROWS, WIDTH), F32),
            pltpu.VMEM((ROWS, WIDTH), BF),
            pltpu.SemaphoreType.DMA((7,)),
            pltpu.SemaphoreType.DMA((1,)),
            pltpu.SemaphoreType.DMA((2,)),
            pltpu.SemaphoreType.DMA((CHUNKS,)),
            pltpu.SemaphoreType.DMA((CHUNKS,)),
            pltpu.SemaphoreType.DMA((37,)),
            pltpu.SemaphoreType.DMA((37,)),
            pltpu.SemaphoreType.DMA((68,)),
            pltpu.SemaphoreType.DMA((68,)),
        ],
        compiler_params=pltpu.CompilerParams(
            collective_id=0, has_side_effects=True, vmem_limit_bytes=56 * 1024 * 1024
        ),
        cost_estimate=pl.CostEstimate(
            flops=3_000_000_000, bytes_accessed=8_000_000, transcendentals=0
        ),
    )(
        adapter_owner_slot, slab_adapter_index, short_filter_taps, long_filter_taps.T,
        adapter_down_weight, adapter_up_weight, projected_queries, projected_keys,
        projected_values, *constants,
    )


def solution(mesh):
    in_specs = (
        P(("group", "ctx"), None),
        P(("group", "ctx"), None),
        P(("group", "ctx"), None),
        P(None, None, "ctx"),
        P(None, "ctx"),
        P("ctx", None, "group"),
        P("ctx", None, "group"),
        P("group", None),
        P(),
    )
    out_specs = P(("group", "ctx"), None)
    return jax.shard_map(
        on_device, mesh=mesh, in_specs=in_specs, out_specs=out_specs, check_vma=False
    )
```
